128 devices in a mesh: wave: 32 (over z, x, core), lat: 4 (over y).
Axes of the slice: x: 4, y: 4, z: 4, core: 2. Of those that a mesh axis runs over, the one named last changes fastest.
Arguments:
- spectral: bfloat16 [2, 64, 2, 2048, 192], P(None, 'wave', None, 'lat'), may hold values from -0.29882812 to 0.29882812
- legendre: bfloat16 [64, 2, 2048, 4096], P('wave', None, None, 'lat'), may hold values from -0.09375 to 0.09375
- wavenumber: int32 [64], replicated, may hold values from 0 to 7999, as said below
Outputs:
- flux: bfloat16 [4, 2048, 512, 128], P('lat', 'wave')
The draws below stay inside these ranges and needn't reach their ends.
Inputs may be any that keep to these rules, and one draw needn't show every extreme that they name: `wavenumber`: the entries come in pairs: entries 2 i and 2 i + 1 are m and 7999 - m with m <= 3999; all entries are distinct, and 0 and 7999 are always present.
All inputs are finite; a program needn't handle non-finite values.
Results may differ from the reference program's by a relative error of at most 0.0066.
Values may be sent and summed in bfloat16 or wider, within the bound.
A program may use at most 128 MiB of HBM per device.

```python
import math
import jax
import jax.numpy as jnp
from jax import lax

TRUNC = 7999
KH = 2048
M = 64
LATH = 1024
LATS = 4096
LEVB = 32
NB = 2
NLONW = 512
N_LAT = 4


def draw_wavenumber(key, part):
    pair_count = M // 2
    shuffled = jax.random.permutation(key, jnp.arange(1, (TRUNC + 1) // 2, dtype=jnp.int32))
    lower = shuffled[:pair_count].at[0].set(0)
    upper = TRUNC - lower
    return jnp.stack([lower, upper], axis=1).reshape(M).astype(jnp.int32)


def shard_levels(key, dims, cuts, least, largest):
    level = 1.0
    for axis_at, blocks in cuts:
        steps = jax.random.uniform(jax.random.fold_in(jax.random.fold_in(key, 6), axis_at), (blocks,), jnp.float32, least / len(cuts), largest / len(cuts))
        level = level * jnp.repeat(jnp.exp(steps), dims[axis_at] // blocks).reshape((-1,) + (1,) * (len(dims) - 1 - axis_at))
    return level


def gaussian(own_key, shape, spread, limit, shards=(), kind=jnp.bfloat16):
    factor_of = shard_levels(own_key, shape, shards, -0.22, 0.18) if shards else 1.0
    values = jax.random.normal(own_key, shape, jnp.float32) * spread * factor_of
    return jnp.minimum(jnp.maximum(values, -limit), limit).astype(kind)


def setup_inputs(seed: int = 0) -> dict:
    seeds = jax.random.split(jax.random.key(seed), 4)
    return {
        "spectral": gaussian(seeds[0], (NB, M, 2, KH, 6 * LEVB), 0.05, 0.29882812, ((1, 32), (3, 4))),
        "legendre": gaussian(seeds[1], (M, 2, KH, LATS), (2 * KH) ** -0.5, 0.09375, ((0, 32), (3, 4))),
        "wavenumber": draw_wavenumber(jax.random.fold_in(seeds[3], 71), 0),
    }


def fourier_table(wavenumber):
    period = 2 * TRUNC + 2
    column = jnp.arange(NLONW, dtype=jnp.int32)
    phase_index = (wavenumber[None, :] * column[:, None]) % period
    angles = phase_index.astype(jnp.float32) * (2.0 * math.pi / period)
    weight = jnp.where(wavenumber == 0, 1.0, 2.0).astype(jnp.float32)
    phase_table = jnp.stack([weight * jnp.cos(angles), -weight * jnp.sin(angles)], axis=2)
    return phase_table.astype(jnp.bfloat16)


def valid_slots(wavenumber, first_slot, slot_count):
    slot_index = first_slot + jnp.arange(slot_count, dtype=jnp.int32)
    parity = jnp.arange(2, dtype=jnp.int32)
    degree = wavenumber[:, None, None] + 2 * slot_index[None, None, :] + parity[None, :, None]
    return degree <= TRUNC


def reference(spectral, legendre, wavenumber):
    valid_mask = valid_slots(wavenumber, 0, KH)
    masked = jnp.where(valid_mask[None, :, :, :, None], spectral, jnp.zeros((), jnp.bfloat16))

    def one_wave(operands):
        poly_rows, coeff_rows = operands
        sums = jnp.einsum("pkl,bpkc->bplc", poly_rows.astype(jnp.float32), coeff_rows.astype(jnp.float32))
        even_sum = sums[:, 0].reshape(NB, N_LAT, LATH, 6 * LEVB)
        odd_sum = sums[:, 1].reshape(NB, N_LAT, LATH, 6 * LEVB)
        return jnp.concatenate([even_sum + odd_sum, even_sum - odd_sum], axis=2).astype(jnp.bfloat16)

    band_values = lax.map(one_wave, (legendre, jnp.swapaxes(masked, 0, 1)))
    phase_table = fourier_table(wavenumber).astype(jnp.float32)
    bands_out = []
    for band_index in range(N_LAT):
        pieces = []
        for batch_index in range(NB):
            spectra = band_values[:, batch_index, band_index].reshape(M, 2 * LATH, 2, 3 * LEVB).astype(jnp.float32)
            grid_values = jnp.einsum("omr,mqrc->qoc", phase_table, spectra)
            vorticity = grid_values[..., :LEVB]
            pieces.append(jnp.concatenate([vorticity * grid_values[..., LEVB:2 * LEVB], vorticity * grid_values[..., 2 * LEVB:]], axis=2))
        bands_out.append(jnp.concatenate(pieces, axis=2).astype(jnp.bfloat16))
    return jnp.stack(bands_out)
```

```python
import functools
import math

import jax
import jax.numpy as jnp
from jax import lax
from jax.experimental import pallas as pl
from jax.experimental.pallas import tpu as pltpu
from jax.sharding import PartitionSpec as P

TRUNC = 7999
NLONW = 512
MESH = pl.DeviceIdType.MESH
F32 = jnp.float32
BF16 = jnp.bfloat16
GROUP = 128


def fourier_table(wavenumber):
    period = 2 * TRUNC + 2
    column = jnp.arange(NLONW, dtype=jnp.int32)
    phase_index = wavenumber[None, :] * column[:, None] % period
    angles = phase_index.astype(F32) * (2.0 * math.pi / period)
    weight = jnp.where(wavenumber == 0, 1.0, 2.0).astype(F32)
    return (weight * jnp.cos(angles)).astype(BF16), (-weight * jnp.sin(angles)).astype(BF16)


def exchange_kernel(
    waves, wn_ref, spec_ref, leg_ref, out_ref,
    spec_v, xg, leg_v, sb,
    spec_sem, leg_sem, own_sem, gs_sem, gr_sem, as_sem, ar_sem,
):
    wave = lax.axis_index("wave")
    lat = lax.axis_index("lat")
    plus, minus = lax.rem(lat + 1, 4), lax.rem(lat + 3, 4)
    batches, slots, _, depth, columns = spec_ref.shape
    levels = columns // 6
    chunks = 3 * slots
    rows = out_ref.shape[2]
    band = leg_ref.shape[3]
    tile = min(256, band)

    def spec_copy(s):
        return pltpu.make_async_copy(spec_ref.at[:, s], spec_v.at[:, s], spec_sem.at[s])

    def leg_copy(s):
        return pltpu.make_async_copy(leg_ref.at[s], leg_v.at[s], leg_sem.at[s])

    for s in range(slots):
        spec_copy(s).start()
    for s in range(slots):
        leg_copy(s).start()

    barrier = pltpu.get_barrier_semaphore()
    for other in (plus, minus):
        pl.semaphore_signal(barrier, inc=1, device_id=(wave, other), device_id_type=MESH)

    def greet(i, carry):
        peer = lax.rem(wave + i, waves)
        pl.semaphore_signal(barrier, inc=1, device_id=(peer, lat), device_id_type=MESH)
        return carry

    lax.fori_loop(1, waves, greet, 0)

    def prepare(s):
        spec_copy(s).wait()
        first = wn_ref[wave * slots + s] + 2 * depth * lat
        slot_index = lax.broadcasted_iota(jnp.int32, (columns, depth), 1)
        for p in range(2):
            live = first + p + 2 * slot_index <= TRUNC
            for b in range(batches):
                turned = spec_v[b, s, p].astype(F32).T
                turned = jnp.where(live, turned, 0.0).astype(BF16)
                at = b * 2 * levels
                for r in range(2):
                    src = r * 3 * levels
                    xg[3 * s, 0, p, at + r * levels : at + (r + 1) * levels, :] = turned[
                        src : src + levels
                    ]
                    xg[3 * s + 1 + r, 0, p, at : at + 2 * levels, :] = turned[
                        src + levels : src + 3 * levels
                    ]

    def gather_copy(g, i):
        src, dst, p, to = (
            (0, 3, 0, plus), (0, 3, 1, plus), (0, 1, 0, minus), (0, 1, 1, minus),
            (3, 2, 0, plus), (1, 2, 1, minus),
        )[i]
        return pltpu.make_async_remote_copy(
            src_ref=xg.at[g, src, p],
            dst_ref=xg.at[g, dst, p],
            send_sem=gs_sem.at[g, i],
            recv_sem=gr_sem.at[g, i],
            device_id=(wave, to),
            device_id_type=MESH,
        )

    def start_own(g):
        for i in (0, 3, 1, 2):
            gather_copy(g, i).start()

    def self_copy(g):
        return pltpu.make_async_copy(sb.at[g, wave], out_ref.at[g, wave], own_sem.at[g])

    def all_of(g):
        peer = lax.rem(wave + 1, waves)
        return pltpu.make_async_remote_copy(
            src_ref=sb.at[g, pl.ds(0, waves - 1)],
            dst_ref=out_ref.at[g, pl.ds(0, waves - 1)],
            send_sem=as_sem.at[g],
            recv_sem=ar_sem.at[g],
            device_id=(peer, lat),
            device_id_type=MESH,
        )

    prepare(0)
    pl.semaphore_wait(barrier, waves + 1)
    start_own(0)
    start_own(1)
    for s in range(1, slots):
        prepare(s)

    def step(g, carry):
        s = g // 3
        gather_copy(g, 0).wait_recv()
        gather_copy(g, 4).start()
        gather_copy(g, 3).wait_recv()
        gather_copy(g, 5).start()

        @pl.when(g + 2 < chunks)
        def _():
            start_own(g + 2)

        for i in (1, 2, 4, 5):
            gather_copy(g, i).wait_recv()

        @pl.when(g == 3 * s)
        def _():
            leg_copy(s).wait()

        def columns_tile(n, inner):
            total = []
            for p in range(2):
                acc = None
                for j in range(4):
                    k0 = pl.multiple_of(lax.rem(lat + j, 4) * depth, depth)
                    poly = leg_v[s, p, pl.ds(k0, depth), pl.ds(pl.multiple_of(n * tile, tile), tile)]
                    part = jnp.dot(xg[g, j, p], poly, preferred_element_type=F32)
                    acc = part if acc is None else acc + part
                total.append(acc)
            per = tile // rows
            north = (total[0] + total[1]).T.astype(BF16)
            south = (total[0] - total[1]).T.astype(BF16)
            sb[g, pl.ds(n * per, per)] = north.reshape(per, rows, GROUP)
            sb[g, pl.ds(waves // 2 + n * per, per)] = south.reshape(per, rows, GROUP)
            return inner

        lax.fori_loop(0, band // tile, columns_tile, 0)

        def send(i, inner):
            peer = lax.rem(wave + i, waves)
            pltpu.make_async_remote_copy(
                src_ref=sb.at[g, peer],
                dst_ref=out_ref.at[g, wave],
                send_sem=as_sem.at[g],
                recv_sem=ar_sem.at[g],
                device_id=(peer, lat),
                device_id_type=MESH,
            ).start()
            return inner

        lax.fori_loop(1, waves, send, 0)
        self_copy(g).start()
        return carry

    lax.fori_loop(0, chunks, step, 0)

    def finish(g, carry):
        for i in range(6):
            gather_copy(g, i).wait_send()
        self_copy(g).wait()
        all_of(g).wait_send()
        all_of(g).wait_recv()
        return carry

    lax.fori_loop(0, chunks, finish, 0)


def synthesis_kernel(waves, block, table_ref, sums_ref, out_ref, wide):
    groups = sums_ref.shape[0]
    levels = GROUP // 4
    wide[...] = sums_ref[...].astype(F32).reshape(groups * waves * block, GROUP)
    lane = lax.broadcasted_iota(jnp.int32, (2 * waves, GROUP), 1)
    real_lane = (lane // levels) % 2 == 0

    def latitude(q, carry):
        def both(t):
            return jnp.concatenate(
                [wide[pl.ds((3 * s + t) * waves * block + q, waves, stride=block), :] for s in range(2)],
                axis=0,
            )

        vort = both(0)
        vort_real = jnp.where(real_lane, vort, pltpu.roll(vort, levels, 1))
        vort_imag = jnp.where(real_lane, pltpu.roll(vort, GROUP - levels, 1), vort)
        rhs = jnp.concatenate(
            [
                jnp.concatenate([vort_real, vort_imag], axis=0),
                jnp.concatenate([both(1), both(2)], axis=0),
            ],
            axis=1,
        ).astype(BF16)
        grid = jnp.dot(table_ref[...], rhs, preferred_element_type=F32)
        out_ref[q] = (grid[:, :GROUP] * grid[:, GROUP:]).astype(BF16)
        return carry

    lax.fori_loop(0, block, latitude, 0, unroll=2)


def shards(waves, spectral, legendre, wavenumber):
    batches, slots, _, depth, columns = spectral.shape
    bands = 4
    band = legendre.shape[3]
    rows = 2 * band // waves
    chunks = 3 * slots
    cosine, sine = fourier_table(wavenumber)
    table = jnp.stack([cosine, sine], axis=1)
    table = table.reshape(NLONW, 2, waves, slots).transpose(0, 1, 3, 2).reshape(NLONW, 2 * slots * waves)

    sums = pl.pallas_call(
        functools.partial(exchange_kernel, waves),
        out_shape=jax.ShapeDtypeStruct((chunks, waves, rows, GROUP), BF16),
        in_specs=[
            pl.BlockSpec(memory_space=pltpu.SMEM),
            pl.BlockSpec(memory_space=pl.ANY),
            pl.BlockSpec(memory_space=pl.ANY),
        ],
        out_specs=pl.BlockSpec(memory_space=pl.ANY),
        scratch_shapes=[
            pltpu.VMEM(spectral.shape, BF16),
            pltpu.VMEM((chunks, bands, 2, GROUP, depth), BF16),
            pltpu.VMEM(legendre.shape, BF16),
            pltpu.VMEM((chunks, waves, rows, GROUP), BF16),
            pltpu.SemaphoreType.DMA((slots,)),
            pltpu.SemaphoreType.DMA((slots,)),
            pltpu.SemaphoreType.DMA((chunks,)),
            pltpu.SemaphoreType.DMA((chunks, 6)),
            pltpu.SemaphoreType.DMA((chunks, 6)),
            pltpu.SemaphoreType.DMA((chunks,)),
            pltpu.SemaphoreType.DMA((chunks,)),
        ],
        compiler_params=pltpu.CompilerParams(
            collective_id=0, has_side_effects=True, vmem_limit_bytes=48 * 1024 * 1024
        ),
        name="gather_sum_exchange",
    )(wavenumber, spectral, legendre)

    block = 16
    flux = pl.pallas_call(
        functools.partial(synthesis_kernel, waves, block),
        grid=(rows // block,),
        out_shape=jax.ShapeDtypeStruct((rows, NLONW, GROUP), BF16),
        in_specs=[
            pl.BlockSpec(table.shape, lambda i: (0, 0)),
            pl.BlockSpec((chunks, waves, block, GROUP), lambda i: (0, 0, i, 0)),
        ],
        out_specs=pl.BlockSpec((block, NLONW, GROUP), lambda i: (i, 0, 0)),
        scratch_shapes=[pltpu.VMEM((chunks * waves * block, GROUP), F32)],
        compiler_params=pltpu.CompilerParams(vmem_limit_bytes=32 * 1024 * 1024),
        name="synthesis_product",
    )(table, sums)
    return flux[None]


def solution(mesh):
    return jax.shard_map(
        functools.partial(shards, mesh.shape["wave"]),
        mesh=mesh,
        in_specs=(P(None, "wave", None, "lat", None), P("wave", None, None, "lat"), P()),
        out_specs=P("lat", "wave", None, None),
        check_vma=False,
    )
```

```python
import functools
import math

import jax
import jax.numpy as jnp
from jax import lax
from jax.experimental import pallas as pl
from jax.experimental.pallas import tpu as pltpu
from jax.sharding import PartitionSpec as P

TRUNC = 7999
NLONW = 512
PERIOD = 2 * TRUNC + 2
MESH = pl.DeviceIdType.MESH
F32 = jnp.float32
BF16 = jnp.bfloat16
BANDS = 4
GROUP = 128


def exchange_kernel(
    waves, wn_hbm, spec_ref, leg_ref, table_ref, held,
    xg, leg_v, sb, rv, wide,
    wn_ref, wn_sem, spec_sem, leg_sem, own_sem, gs_sem, gr_sem, as_sem, ar_sem,
):
    wave = lax.axis_index("wave")
    lat = lax.axis_index("lat")
    plus, minus = lax.rem(lat + 1, BANDS), lax.rem(lat + BANDS - 1, BANDS)
    batches, slots, _, columns, depth = spec_ref.shape
    levels = columns // 6
    chunks = 3 * slots
    rows = rv.shape[2]
    band = leg_ref.shape[3]
    tile = min(256, band)
    tiles = band // tile
    per = tile // rows
    half = waves // 2

    def spec_copies(s):
        copies = []
        for p in range(2):
            for b in range(batches):
                at = b * 2 * levels
                for r in range(2):
                    src = r * 3 * levels
                    copies.append((3 * s, p, at + r * levels, b, src, levels))
                    copies.append((3 * s + 1 + r, p, at, b, src + levels, 2 * levels))
        return [
            pltpu.make_async_copy(
                spec_ref.at[b, s, p, pl.ds(src, count)],
                xg.at[g, 0, p, pl.ds(dst, count)],
                spec_sem.at[s, n],
            )
            for n, (g, p, dst, b, src, count) in enumerate(copies)
        ]

    def leg_copy(s):
        return pltpu.make_async_copy(leg_ref.at[s], leg_v.at[s], leg_sem.at[s])

    numbers = pltpu.make_async_copy(wn_hbm, wn_ref, wn_sem)
    numbers.start()
    for s in range(slots):
        for copy in spec_copies(s):
            copy.start()

    barrier = pltpu.get_barrier_semaphore()
    for other in (plus, minus):
        pl.semaphore_signal(barrier, inc=1, device_id=(wave, other), device_id_type=MESH)

    def greet(i, carry):
        peer = lax.rem(wave + i, waves)
        pl.semaphore_signal(barrier, inc=1, device_id=(peer, lat), device_id_type=MESH)
        return carry

    lax.fori_loop(1, waves, greet, 0)
    for s in range(slots):
        leg_copy(s).start()

    def prepare(s):
        for copy in spec_copies(s):
            copy.wait()
        first = wn_ref[wave * slots + s] + 2 * depth * lat
        slot_index = lax.broadcasted_iota(jnp.int32, (GROUP, depth), 1)
        for p in range(2):
            live = first + p + 2 * slot_index <= TRUNC
            for t in range(3):
                g = 3 * s + t
                xg[g, 0, p] = jnp.where(live, xg[g, 0, p].astype(F32), 0.0).astype(BF16)

    def gather_copy(g, i):
        src, dst, p, to = (
            (0, 3, 0, plus), (0, 3, 1, plus), (0, 1, 0, minus), (0, 1, 1, minus),
            (3, 2, 0, plus), (1, 2, 1, minus),
        )[i]
        return pltpu.make_async_remote_copy(
            src_ref=xg.at[g, src, p],
            dst_ref=xg.at[g, dst, p],
            send_sem=gs_sem.at[g, i],
            recv_sem=gr_sem.at[g, i],
            device_id=(wave, to),
            device_id_type=MESH,
        )

    def start_own(g):
        for i in (0, 3, 1, 2):
            gather_copy(g, i).start()

    def self_copy(g):
        return pltpu.make_async_copy(sb.at[g, wave], rv.at[g, wave], own_sem.at[g])

    def all_of(g):
        peer = lax.rem(wave + 1, waves)
        return pltpu.make_async_remote_copy(
            src_ref=sb.at[g, pl.ds(0, waves - 1)],
            dst_ref=rv.at[g, pl.ds(0, waves - 1)],
            send_sem=as_sem.at[g],
            recv_sem=ar_sem.at[g],
            device_id=(peer, lat),
            device_id_type=MESH,
        )

    def make_table():
        lane = lax.broadcasted_iota(jnp.int32, (8, 2 * slots * waves), 1)
        slot = slots * lax.rem(lane, waves) + lax.rem(lane // waves, slots)
        number = jnp.zeros_like(lane)
        for n in range(slots * waves):
            number = jnp.where(slot == n, wn_ref[n], number)
        weight = jnp.where(number == 0, 1.0, 2.0).astype(F32)
        real = lane < slots * waves

        def block(i, carry):
            column = lax.broadcasted_iota(jnp.int32, lane.shape, 0)
            parts = []
            for n in range(2):
                product = number * (column + (16 * i + 8 * n))
                turns = jnp.floor(product.astype(F32) * (1.0 / PERIOD)).astype(jnp.int32)
                phase = product - turns * PERIOD
                phase = jnp.where(phase < 0, phase + PERIOD, phase)
                phase = jnp.where(phase >= PERIOD, phase - PERIOD, phase)
                angle = phase.astype(F32) * (2.0 * math.pi / PERIOD)
                parts.append(jnp.where(real, weight * jnp.cos(angle), -weight * jnp.sin(angle)))
            table_ref[pl.ds(pl.multiple_of(16 * i, 16), 16), :] = jnp.concatenate(parts, axis=0).astype(BF16)
            return carry

        lax.fori_loop(0, NLONW // 16, block, 0)

    def arrange(g):
        s = g // 3
        t = g - 3 * s
        all_of(g).wait_recv()
        self_copy(g).wait()
        wide[...] = rv[g].astype(F32).reshape(waves * rows, GROUP)
        lane = lax.broadcasted_iota(jnp.int32, (waves, GROUP), 1)
        real_lane = lax.rem(lane // levels, 2) == 0

        @pl.when(t == 0)
        def _():
            def latitude(q, carry):
                x = wide[pl.ds(q, waves, stride=rows), :]
                real = jnp.where(real_lane, x, pltpu.roll(x, levels, 1))
                imag = jnp.where(real_lane, pltpu.roll(x, GROUP - levels, 1), x)
                held[q, pl.ds(s * waves, waves), 0:GROUP] = real.astype(BF16)
                held[q, pl.ds((slots + s) * waves, waves), 0:GROUP] = imag.astype(BF16)
                return carry

            lax.fori_loop(0, rows, latitude, 0, unroll=8)

        @pl.when(t > 0)
        def _():
            r = t - 1

            def latitude(q, carry):
                x = wide[pl.ds(q, waves, stride=rows), :]
                held[q, pl.ds((r * slots + s) * waves, waves), GROUP : 2 * GROUP] = x.astype(BF16)
                return carry

            lax.fori_loop(0, rows, latitude, 0, unroll=8)

    numbers.wait()
    prepare(0)
    pl.semaphore_wait(barrier, waves + 1)
    start_own(0)
    for s in range(1, slots):
        prepare(s)
    make_table()

    def step(g, carry):
        s = g // 3
        gather_copy(g, 0).wait_recv()
        gather_copy(g, 4).start()
        gather_copy(g, 3).wait_recv()
        gather_copy(g, 5).start()

        @pl.when(g + 1 < chunks)
        def _():
            start_own(g + 1)

        @pl.when(g >= 2)
        def _():
            arrange(g - 2)

        for i in (1, 2, 4, 5):
            gather_copy(g, i).wait_recv()

        @pl.when(g == 3 * s)
        def _():
            leg_copy(s).wait()

        def columns_tile(turn, inner):
            n = lax.rem(turn + wave, tiles)
            total = []
            for p in range(2):
                acc = None
                for j in range(BANDS):
                    k0 = pl.multiple_of(lax.rem(lat + j, BANDS) * depth, depth)
                    poly = leg_v[s, p, pl.ds(k0, depth), pl.ds(pl.multiple_of(n * tile, tile), tile)]
                    part = jnp.dot(xg[g, j, p], poly, preferred_element_type=F32)
                    acc = part if acc is None else acc + part
                total.append(acc)
            north = (total[0] + total[1]).T.astype(BF16)
            south = (total[0] - total[1]).T.astype(BF16)
            sb[g, pl.ds(n * per, per)] = north.reshape(per, rows, GROUP)
            sb[g, pl.ds(half + n * per, per)] = south.reshape(per, rows, GROUP)

            def send(i, after):
                peer = n * per + lax.rem(i, per) + half * (i // per)

                @pl.when(peer != wave)
                def _():
                    pltpu.make_async_remote_copy(
                        src_ref=sb.at[g, peer],
                        dst_ref=rv.at[g, wave],
                        send_sem=as_sem.at[g],
                        recv_sem=ar_sem.at[g],
                        device_id=(peer, lat),
                        device_id_type=MESH,
                    ).start()

                return after

            lax.fori_loop(0, 2 * per, send, 0)
            return inner

        lax.fori_loop(0, tiles, columns_tile, 0)
        self_copy(g).start()
        return carry

    lax.fori_loop(0, chunks, step, 0)
    for g in range(chunks - 2, chunks):
        arrange(g)

    def finish(g, carry):
        for i in range(6):
            gather_copy(g, i).wait_send()
        all_of(g).wait_send()
        return carry

    lax.fori_loop(0, chunks, finish, 0)


def synthesis_kernel(block, table_ref, rhs_ref, out_ref):
    first = pl.program_id(0) * block
    for q in range(block):
        grid = jnp.dot(table_ref[...], rhs_ref[first + q], preferred_element_type=F32)
        out_ref[q] = (grid[:, :GROUP] * grid[:, GROUP:]).astype(BF16)


def shards(waves, spectral, legendre, wavenumber):
    spectral = jnp.swapaxes(spectral, 3, 4)
    slots = spectral.shape[1]
    depth = spectral.shape[4]
    rows = 2 * legendre.shape[3] // waves
    chunks = 3 * slots
    inner = 2 * slots * waves

    table, rhs = pl.pallas_call(
        functools.partial(exchange_kernel, waves),
        out_shape=[
            jax.ShapeDtypeStruct((NLONW, inner), BF16),
            jax.ShapeDtypeStruct((rows, inner, 2 * GROUP), BF16),
        ],
        in_specs=[
            pl.BlockSpec(memory_space=pl.ANY),
            pl.BlockSpec(memory_space=pl.ANY),
            pl.BlockSpec(memory_space=pl.ANY),
        ],
        out_specs=[pl.BlockSpec(memory_space=pltpu.VMEM)] * 2,
        scratch_shapes=[
            pltpu.VMEM((chunks, BANDS, 2, GROUP, depth), BF16),
            pltpu.VMEM(legendre.shape, BF16),
            pltpu.VMEM((chunks, waves, rows, GROUP), BF16),
            pltpu.VMEM((chunks, waves, rows, GROUP), BF16),
            pltpu.VMEM((waves * rows, GROUP), F32),
            pltpu.SMEM((slots * waves,), jnp.int32),
            pltpu.SemaphoreType.DMA,
            pltpu.SemaphoreType.DMA((slots, 16)),
            pltpu.SemaphoreType.DMA((slots,)),
            pltpu.SemaphoreType.DMA((chunks,)),
            pltpu.SemaphoreType.DMA((chunks, 6)),
            pltpu.SemaphoreType.DMA((chunks, 6)),
            pltpu.SemaphoreType.DMA((chunks,)),
            pltpu.SemaphoreType.DMA((chunks,)),
        ],
        compiler_params=pltpu.CompilerParams(
            collective_id=0, has_side_effects=True, vmem_limit_bytes=42 * 1024 * 1024
        ),
        name="gather_sum_exchange",
    )(wavenumber, spectral, legendre)

    block = 8
    flux = pl.pallas_call(
        functools.partial(synthesis_kernel, block),
        grid=(rows // block,),
        out_shape=jax.ShapeDtypeStruct((rows, NLONW, GROUP), BF16),
        in_specs=[
            pl.BlockSpec(memory_space=pltpu.VMEM),
            pl.BlockSpec(memory_space=pltpu.VMEM),
        ],
        out_specs=pl.BlockSpec((block, NLONW, GROUP), lambda i: (i, 0, 0)),
        compiler_params=pltpu.CompilerParams(vmem_limit_bytes=24 * 1024 * 1024),
        name="synthesis_product",
    )(table, rhs)
    return flux[None]


def solution(mesh):
    return jax.shard_map(
        functools.partial(shards, mesh.shape["wave"]),
        mesh=mesh,
        in_specs=(P(None, "wave", None, "lat", None), P("wave", None, None, "lat"), P()),
        out_specs=P("lat", "wave", None, None),
        check_vma=False,
    )
```

```python
import functools
import math

import jax
import jax.numpy as jnp
from jax import lax
from jax.experimental import pallas as pl
from jax.experimental.pallas import tpu as pltpu
from jax.sharding import PartitionSpec as P

TRUNC = 7999
NLONW = 512
PERIOD = 2 * TRUNC + 2
MESH = pl.DeviceIdType.MESH
F32 = jnp.float32
BF16 = jnp.bfloat16
BANDS = 4
GROUP = 128


def exchange_kernel(
    waves, wn_hbm, spec_ref, leg_ref, table_ref, rhs_ref,
    xg, leg_v, sb, rv, wide, partial, wn_ref,
    wn_sem, leg_sem, own_sem, gs_sem, gr_sem, as_sem, ar_sem,
):
    wave = lax.axis_index("wave")
    lat = lax.axis_index("lat")
    plus, minus = lax.rem(lat + 1, BANDS), lax.rem(lat + BANDS - 1, BANDS)
    batches, slots, _, columns, depth = spec_ref.shape
    levels = columns // 6
    full = 3 * slots - 1
    rows = rv.shape[2]
    short = rows // 2
    narrow = GROUP // 2
    band = leg_ref.shape[3]
    tile = min(256, band)
    tiles = band // tile
    per = tile // rows
    half = waves // 2

    numbers = pltpu.make_async_copy(wn_hbm, wn_ref, wn_sem)
    numbers.start()

    def leg_copy(s):
        return pltpu.make_async_copy(leg_ref.at[s], leg_v.at[s], leg_sem.at[s])

    barrier = pltpu.get_barrier_semaphore()
    for other in (plus, minus):
        pl.semaphore_signal(barrier, inc=1, device_id=(wave, other), device_id_type=MESH)

    def greet(i, carry):
        peer = lax.rem(wave + i, waves)
        pl.semaphore_signal(barrier, inc=1, device_id=(peer, lat), device_id_type=MESH)
        return carry

    lax.fori_loop(1, waves, greet, 0)
    for s in range(slots):
        leg_copy(s).start()

    def prepare(s):
        first = wn_ref[wave * slots + s] + 2 * depth * lat
        slot_index = lax.broadcasted_iota(jnp.int32, (2 * levels, depth), 1)
        for p in range(2):
            live = first + p + 2 * slot_index <= TRUNC
            for b in range(batches):
                at = b * 2 * levels
                for r in range(2):
                    src = r * 3 * levels
                    vort = spec_ref[b, s, p, src : src + levels].astype(F32)
                    xg[s, 0, p, at + r * levels : at + (r + 1) * levels] = jnp.where(
                        live[:levels], vort, 0.0
                    ).astype(BF16)
                    wind = spec_ref[b, s, p, src + levels : src + 3 * levels].astype(F32)
                    xg[(1 + r) * slots + s, 0, p, at : at + 2 * levels] = jnp.where(live, wind, 0.0).astype(BF16)

    def gather_copy(g, i, part=None):
        src, dst, p, to = (
            (0, 3, 0, plus), (0, 3, 1, plus), (0, 1, 0, minus), (0, 1, 1, minus),
            (3, 2, 0, plus), (1, 2, 1, minus),
        )[i]
        piece = pl.ds(0, GROUP) if part is None else pl.ds(part * narrow, narrow)
        at = g if part is None else g + part
        return pltpu.make_async_remote_copy(
            src_ref=xg.at[g, src, p, piece],
            dst_ref=xg.at[g, dst, p, piece],
            send_sem=gs_sem.at[at, i],
            recv_sem=gr_sem.at[at, i],
            device_id=(wave, to),
            device_id_type=MESH,
        )

    def start_own(g, part=None):
        for i in (0, 3, 1, 2):
            gather_copy(g, i, part).start()

    def lines(part):
        return pl.ds(0, rows) if part is None else pl.ds(part * short, short)

    def self_copy(g, part=None):
        return pltpu.make_async_copy(
            sb.at[g, wave, lines(part)], rv.at[g, wave, lines(part)], own_sem.at[g + (part or 0)]
        )

    def all_of(g, part=None):
        peer = lax.rem(wave + 1, waves)
        return pltpu.make_async_remote_copy(
            src_ref=sb.at[g, pl.ds(0, waves - 1), lines(part)],
            dst_ref=rv.at[g, pl.ds(0, waves - 1), lines(part)],
            send_sem=as_sem.at[g + (part or 0)],
            recv_sem=ar_sem.at[g + (part or 0)],
            device_id=(peer, lat),
            device_id_type=MESH,
        )

    def make_table():
        lane = lax.broadcasted_iota(jnp.int32, (8, 2 * slots * waves), 1)
        slot = slots * lax.rem(lane, waves) + lax.rem(lane // waves, slots)
        number = jnp.zeros_like(lane)
        for n in range(slots * waves):
            number = jnp.where(slot == n, wn_ref[n], number)
        weight = jnp.where(number == 0, 1.0, 2.0).astype(F32)
        real = lane < slots * waves

        def block(i, carry):
            column = lax.broadcasted_iota(jnp.int32, lane.shape, 0)
            parts = []
            for n in range(2):
                product = number * (column + (16 * i + 8 * n))
                turns = jnp.floor(product.astype(F32) * (1.0 / PERIOD)).astype(jnp.int32)
                phase = product - turns * PERIOD
                phase = jnp.where(phase < 0, phase + PERIOD, phase)
                phase = jnp.where(phase >= PERIOD, phase - PERIOD, phase)
                angle = phase.astype(F32) * (2.0 * math.pi / PERIOD)
                parts.append(jnp.where(real, weight * jnp.cos(angle), -weight * jnp.sin(angle)))
            table_ref[pl.ds(pl.multiple_of(16 * i, 16), 16), :] = jnp.concatenate(parts, axis=0).astype(BF16)
            return carry

        lax.fori_loop(0, NLONW // 16, block, 0)

    def arrange(g):
        s = lax.rem(g, slots)
        t = g // slots
        all_of(g).wait_recv()
        self_copy(g).wait()
        wide[...] = rv[g].astype(F32).reshape(waves * rows, GROUP)

        @pl.when(t == 0)
        def _():
            lane = lax.broadcasted_iota(jnp.int32, (waves, GROUP), 1)
            real_lane = lax.rem(lane // levels, 2) == 0

            def latitude(q, carry):
                x = wide[pl.ds(q, waves, stride=rows), :]
                real = jnp.where(real_lane, x, pltpu.roll(x, levels, 1))
                imag = jnp.where(real_lane, pltpu.roll(x, GROUP - levels, 1), x)
                rhs_ref[q, pl.ds(s * waves, waves), 0:GROUP] = real.astype(BF16)
                rhs_ref[q, pl.ds((slots + s) * waves, waves), 0:GROUP] = imag.astype(BF16)
                return carry

            lax.fori_loop(0, rows, latitude, 0, unroll=8)

        @pl.when(t > 0)
        def _():
            def latitude(q, carry):
                x = wide[pl.ds(q, waves, stride=rows), :]
                rhs_ref[q, pl.ds((g - slots) * waves, waves), GROUP : 2 * GROUP] = x.astype(BF16)
                return carry

            lax.fori_loop(0, rows, latitude, 0, unroll=8)

    def arrange_half(part):
        all_of(full, part).wait_recv()
        self_copy(full, part).wait()
        wide[0 : waves * short] = rv[full, :, part * short : (part + 1) * short].astype(F32).reshape(
            waves * short, GROUP
        )
        at = pl.ds((full - slots) * waves, waves)

        def latitude(q, carry):
            x = wide[pl.ds(q, waves, stride=short), :]
            turned = pltpu.roll(x, narrow, 1)
            first, second = (x, turned) if part == 0 else (turned, x)
            cut = slice(part * narrow, (part + 1) * narrow)
            into = slice(GROUP + part * narrow, GROUP + (part + 1) * narrow)
            rhs_ref[q, at, into] = first[:, cut].astype(BF16)
            rhs_ref[q + short, at, into] = second[:, cut].astype(BF16)
            return carry

        lax.fori_loop(0, short, latitude, 0, unroll=8)

    def product(g, s, part, n, sources):
        piece = slice(0, GROUP) if part is None else slice(part * narrow, (part + 1) * narrow)
        total = []
        for p in range(2):
            acc = None
            for j in sources:
                k0 = pl.multiple_of(lax.rem(lat + j, BANDS) * depth, depth)
                poly = leg_v[s, p, pl.ds(k0, depth), pl.ds(pl.multiple_of(n * tile, tile), tile)]
                add = jnp.dot(xg[g, j, p, piece], poly, preferred_element_type=F32)
                acc = add if acc is None else acc + add
            total.append(acc)
        return total

    def begin(g, s, part):
        for i in (1, 2):
            gather_copy(g, i, part).wait_recv()

        def columns_tile(n, inner):
            partial[n, 0], partial[n, 1] = product(g, s, part, n, (0, 1, 3))
            return inner

        lax.fori_loop(0, tiles, columns_tile, 0)
        for i in (4, 5):
            gather_copy(g, i, part).wait_recv()

    def multiply(g, s, part=None):
        def columns_tile(turn, inner):
            n = lax.rem(turn + wave, tiles)
            if part is None:
                total = product(g, s, part, n, (0, 1, 3, 2))
            else:
                total = product(g, s, part, n, (2,))
                total = [total[p] + partial[n, p] for p in range(2)]
            for at, value in ((0, total[0] + total[1]), (half, total[0] - total[1])):
                if part is None:
                    sb[g, pl.ds(at + n * per, per)] = value.T.astype(BF16).reshape(per, rows, GROUP)
                else:
                    turned = value.T.reshape(per, rows, narrow)
                    packed = jnp.concatenate([turned[:, :short], turned[:, short:]], axis=2)
                    sb[g, pl.ds(at + n * per, per), part * short : (part + 1) * short] = packed.astype(BF16)

            def send(i, after):
                peer = n * per + lax.rem(i, per) + half * (i // per)

                @pl.when(peer != wave)
                def _():
                    pltpu.make_async_remote_copy(
                        src_ref=sb.at[g, peer, lines(part)],
                        dst_ref=rv.at[g, wave, lines(part)],
                        send_sem=as_sem.at[g + (part or 0)],
                        recv_sem=ar_sem.at[g + (part or 0)],
                        device_id=(peer, lat),
                        device_id_type=MESH,
                    ).start()

                return after

            lax.fori_loop(0, 2 * per, send, 0)
            return inner

        lax.fori_loop(0, tiles, columns_tile, 0)
        self_copy(g, part).start()

    def hand_on(g, part=None):
        gather_copy(g, 0, part).wait_recv()
        gather_copy(g, 4, part).start()
        gather_copy(g, 3, part).wait_recv()
        gather_copy(g, 5, part).start()

    def rest(g, part=None):
        for i in (1, 2, 4, 5):
            gather_copy(g, i, part).wait_recv()

    numbers.wait()
    prepare(0)
    pl.semaphore_wait(barrier, waves + 1)
    start_own(0)
    for s in range(1, slots):
        prepare(s)
    make_table()
    hand_on(0)
    start_own(1)

    def step(g, carry):
        @pl.when(g + 1 < full)
        def _():
            hand_on(g + 1)

        @pl.when(g + 2 < full)
        def _():
            start_own(g + 2)

        @pl.when(g + 2 == full)
        def _():
            start_own(full, 0)

        @pl.when(g + 1 == full)
        def _():
            hand_on(full, 0)
            start_own(full, 1)

        rest(g)

        @pl.when(g < slots)
        def _():
            leg_copy(g).wait()

        multiply(g, lax.rem(g, slots))

        @pl.when((g >= 2) & (g < full - 1))
        def _():
            arrange(g - 2)

        return carry

    lax.fori_loop(0, full, step, 0)
    begin(full, slots - 1, 0)
    hand_on(full, 1)
    multiply(full, slots - 1, 0)
    begin(full, slots - 1, 1)
    multiply(full, slots - 1, 1)
    for g in (full - 3, full - 2, full - 1):
        arrange(g)
    for part in range(2):
        arrange_half(part)

    def finish(g, carry):
        for i in range(6):
            gather_copy(g, i).wait_send()
        all_of(g).wait_send()
        return carry

    lax.fori_loop(0, full, finish, 0)
    for part in range(2):
        for i in range(6):
            gather_copy(full, i, part).wait_send()
        all_of(full, part).wait_send()


def synthesis_kernel(block, table_ref, rhs_ref, out_ref, made, out_sem):
    rows = rhs_ref.shape[0]

    def out_copy(i):
        piece = pl.ds(i * 8, 8)
        return pltpu.make_async_copy(made.at[piece], out_ref.at[piece], out_sem.at[i])

    def step(i, carry):
        for n in range(block):
            q = i * block + n
            grid = jnp.dot(table_ref[...], rhs_ref[q], preferred_element_type=F32)
            made[q] = (grid[:, :GROUP] * grid[:, GROUP:]).astype(BF16)
            if n % 8 == 8-1:
                out_copy(n // 8).start()
        return carry

    lax.fori_loop(0, rows // block, step, 0)

    def finish(i, carry):
        out_copy(i).wait()
        return carry

    lax.fori_loop(0, rows // 8, finish, 0)


def shards(waves, spectral, legendre, wavenumber):
    spectral = jnp.swapaxes(spectral, 3, 4)
    slots = spectral.shape[1]
    depth = spectral.shape[4]
    rows = 2 * legendre.shape[3] // waves
    band = legendre.shape[3]
    tiles = max(1, band // 256)
    chunks = 3 * slots
    inner = 2 * slots * waves

    table, rhs = pl.pallas_call(
        functools.partial(exchange_kernel, waves),
        out_shape=[
            jax.ShapeDtypeStruct((NLONW, inner), BF16),
            jax.ShapeDtypeStruct((rows, inner, 2 * GROUP), BF16),
        ],
        in_specs=[
            pl.BlockSpec(memory_space=pl.ANY),
            pl.BlockSpec(memory_space=pltpu.VMEM),
            pl.BlockSpec(memory_space=pl.ANY),
        ],
        out_specs=[pl.BlockSpec(memory_space=pltpu.VMEM)] * 2,
        scratch_shapes=[
            pltpu.VMEM((chunks, BANDS, 2, GROUP, depth), BF16),
            pltpu.VMEM(legendre.shape, BF16),
            pltpu.VMEM((chunks, waves, rows, GROUP), BF16),
            pltpu.VMEM((chunks, waves, rows, GROUP), BF16),
            pltpu.VMEM((waves * rows, GROUP), F32),
            pltpu.VMEM((tiles, 2, GROUP // 2, band // tiles), F32),
            pltpu.SMEM((slots * waves,), jnp.int32),
            pltpu.SemaphoreType.DMA,
            pltpu.SemaphoreType.DMA((slots,)),
            pltpu.SemaphoreType.DMA((chunks + 1,)),
            pltpu.SemaphoreType.DMA((chunks + 1, 6)),
            pltpu.SemaphoreType.DMA((chunks + 1, 6)),
            pltpu.SemaphoreType.DMA((chunks + 1,)),
            pltpu.SemaphoreType.DMA((chunks + 1,)),
        ],
        compiler_params=pltpu.CompilerParams(
            collective_id=0, has_side_effects=True, vmem_limit_bytes=36 * 1024 * 1024
        ),
        name="gather_sum_exchange",
    )(wavenumber, spectral, legendre)

    block = 64
    flux = pl.pallas_call(
        functools.partial(synthesis_kernel, block),
        out_shape=jax.ShapeDtypeStruct((rows, NLONW, GROUP), BF16),
        in_specs=[pl.BlockSpec(memory_space=pltpu.VMEM)] * 2,
        out_specs=pl.BlockSpec(memory_space=pl.ANY),
        scratch_shapes=[
            pltpu.VMEM((rows, NLONW, GROUP), BF16),
            pltpu.SemaphoreType.DMA((rows // 8,)),
        ],
        compiler_params=pltpu.CompilerParams(vmem_limit_bytes=24 * 1024 * 1024),
        name="synthesis_product",
    )(table, rhs)
    return flux[None]


def solution(mesh):
    return jax.shard_map(
        functools.partial(shards, mesh.shape["wave"]),
        mesh=mesh,
        in_specs=(P(None, "wave", None, "lat", None), P("wave", None, None, "lat"), P()),
        out_specs=P("lat", "wave", None, None),
        check_vma=False,
    )
```

```python
import functools
import math

import jax
import jax.numpy as jnp
from jax import lax
from jax.experimental import pallas as pl
from jax.experimental.pallas import tpu as pltpu
from jax.sharding import PartitionSpec as P

TRUNC = 7999
NLONW = 512
PERIOD = 2 * TRUNC + 2
MESH = pl.DeviceIdType.MESH
F32 = jnp.float32
BF16 = jnp.bfloat16
BANDS = 4
GROUP = 128


def exchange_kernel(
    waves, wn_hbm, spec_ref, leg_ref, table_ref, wind_ref, vort_ref,
    xg, leg_v, sb, rv, wide, early, early_last, held, wn_ref,
    wn_sem, leg_sem, own_sem, gs_sem, gr_sem, as_sem, ar_sem,
):
    wave = lax.axis_index("wave")
    lat = lax.axis_index("lat")
    plus, minus = lax.rem(lat + 1, BANDS), lax.rem(lat + BANDS - 1, BANDS)
    batches, slots, _, columns, depth = spec_ref.shape
    levels = columns // 6
    full = 3 * slots - 1
    rows = rv.shape[2]
    short = rows // 2
    narrow = GROUP // 2
    band = leg_ref.shape[3]
    tile = min(256, band)
    tiles = band // tile
    per = tile // rows
    half = waves // 2

    numbers = pltpu.make_async_copy(wn_hbm, wn_ref, wn_sem)
    numbers.start()

    def leg_copy(s):
        return pltpu.make_async_copy(leg_ref.at[s], leg_v.at[s], leg_sem.at[s])

    barrier = pltpu.get_barrier_semaphore()
    for other in (plus, minus):
        pl.semaphore_signal(barrier, inc=1, device_id=(wave, other), device_id_type=MESH)

    def greet(i, carry):
        peer = lax.rem(wave + i, waves)
        pl.semaphore_signal(barrier, inc=1, device_id=(peer, lat), device_id_type=MESH)
        return carry

    lax.fori_loop(1, waves, greet, 0)
    for s in range(slots):
        leg_copy(s).start()

    def prepare(s):
        first = wn_ref[wave * slots + s] + 2 * depth * lat
        slot_index = lax.broadcasted_iota(jnp.int32, (2 * levels, depth), 1)
        for p in range(2):
            live = first + p + 2 * slot_index <= TRUNC
            for b in range(batches):
                at = b * 2 * levels
                for r in range(2):
                    src = r * 3 * levels
                    vort = spec_ref[b, s, p, src : src + levels].astype(F32)
                    xg[s, 0, p, at + r * levels : at + (r + 1) * levels] = jnp.where(
                        live[:levels], vort, 0.0
                    ).astype(BF16)
                    wind = spec_ref[b, s, p, src + levels : src + 3 * levels].astype(F32)
                    xg[(1 + r) * slots + s, 0, p, at : at + 2 * levels] = jnp.where(live, wind, 0.0).astype(BF16)

    def gather_copy(g, i, part=None):
        src, dst, p, to = (
            (0, 3, 0, plus), (0, 3, 1, plus), (0, 1, 0, minus), (0, 1, 1, minus),
            (3, 2, 0, plus), (1, 2, 1, minus),
        )[i]
        piece = pl.ds(0, GROUP) if part is None else pl.ds(part * narrow, narrow)
        at = g if part is None else g + part
        return pltpu.make_async_remote_copy(
            src_ref=xg.at[g, src, p, piece],
            dst_ref=xg.at[g, dst, p, piece],
            send_sem=gs_sem.at[at, i],
            recv_sem=gr_sem.at[at, i],
            device_id=(wave, to),
            device_id_type=MESH,
        )

    def start_own(g, part=None):
        for i in (0, 3, 1, 2):
            gather_copy(g, i, part).start()

    def lines(part):
        return pl.ds(0, rows) if part is None else pl.ds(part * short, short)

    def self_copy(g, part=None):
        return pltpu.make_async_copy(
            sb.at[g, wave, lines(part)], rv.at[g, wave, lines(part)], own_sem.at[g + (part or 0)]
        )

    def all_of(g, part=None):
        peer = lax.rem(wave + 1, waves)
        return pltpu.make_async_remote_copy(
            src_ref=sb.at[g, pl.ds(0, waves - 1), lines(part)],
            dst_ref=rv.at[g, pl.ds(0, waves - 1), lines(part)],
            send_sem=as_sem.at[g + (part or 0)],
            recv_sem=ar_sem.at[g + (part or 0)],
            device_id=(peer, lat),
            device_id_type=MESH,
        )

    def make_table():
        lane = lax.broadcasted_iota(jnp.int32, (8, 2 * slots * waves), 1)
        slot = slots * lax.rem(lane, waves) + lax.rem(lane // waves, slots)
        number = jnp.zeros_like(lane)
        for n in range(slots * waves):
            number = jnp.where(slot == n, wn_ref[n], number)
        weight = jnp.where(number == 0, 1.0, 2.0).astype(F32)
        real = lane < slots * waves

        def block(i, carry):
            column = lax.broadcasted_iota(jnp.int32, lane.shape, 0)
            parts = []
            for n in range(2):
                product = number * (column + (16 * i + 8 * n))
                turns = jnp.floor(product.astype(F32) * (1.0 / PERIOD)).astype(jnp.int32)
                phase = product - turns * PERIOD
                phase = jnp.where(phase < 0, phase + PERIOD, phase)
                phase = jnp.where(phase >= PERIOD, phase - PERIOD, phase)
                angle = phase.astype(F32) * (2.0 * math.pi / PERIOD)
                parts.append(jnp.where(real, weight * jnp.cos(angle), -weight * jnp.sin(angle)))
            table_ref[pl.ds(pl.multiple_of(16 * i, 16), 16), :] = jnp.concatenate(parts, axis=0).astype(BF16)
            return carry

        lax.fori_loop(0, NLONW // 16, block, 0)

    def arrange(g):
        s = lax.rem(g, slots)
        t = g // slots
        all_of(g).wait_recv()
        self_copy(g).wait()
        wide[...] = rv[g].astype(F32).reshape(waves * rows, GROUP)

        @pl.when(t == 0)
        def _():
            lane = lax.broadcasted_iota(jnp.int32, (waves, GROUP), 1)
            real_lane = lax.rem(lane // levels, 2) == 0

            def latitude(q, carry):
                x = wide[pl.ds(q, waves, stride=rows), :]
                real = jnp.where(real_lane, x, pltpu.roll(x, levels, 1))
                imag = jnp.where(real_lane, pltpu.roll(x, GROUP - levels, 1), x)
                held[q, pl.ds(s * waves, waves), :] = real.astype(BF16)
                held[q, pl.ds((slots + s) * waves, waves), :] = imag.astype(BF16)
                return carry

            lax.fori_loop(0, rows, latitude, 0, unroll=8)

        @pl.when(t > 0)
        def _():
            def latitude(q, carry):
                x = wide[pl.ds(q, waves, stride=rows), :]
                wind_ref[q, pl.ds((g - slots) * waves, waves), :] = x.astype(BF16)
                return carry

            lax.fori_loop(0, rows, latitude, 0, unroll=8)

    def arrange_half(part):
        all_of(full, part).wait_recv()
        self_copy(full, part).wait()
        wide[0 : waves * short] = rv[full, :, part * short : (part + 1) * short].astype(F32).reshape(
            waves * short, GROUP
        )
        at = pl.ds((full - slots) * waves, waves)

        def latitude(q, carry):
            x = wide[pl.ds(q, waves, stride=short), :]
            turned = pltpu.roll(x, narrow, 1)
            first, second = (x, turned) if part == 0 else (turned, x)
            cut = slice(part * narrow, (part + 1) * narrow)
            wind_ref[q, at, cut] = first[:, cut].astype(BF16)
            wind_ref[q + short, at, cut] = second[:, cut].astype(BF16)
            return carry

        lax.fori_loop(0, short, latitude, 0, unroll=8)

    def product(g, s, part, n, sources):
        piece = slice(0, GROUP) if part is None else slice(part * narrow, (part + 1) * narrow)
        total = []
        for p in range(2):
            acc = None
            for j in sources:
                k0 = pl.multiple_of(lax.rem(lat + j, BANDS) * depth, depth)
                poly = leg_v[s, p, pl.ds(k0, depth), pl.ds(pl.multiple_of(n * tile, tile), tile)]
                add = jnp.dot(xg[g, j, p, piece], poly, preferred_element_type=F32)
                acc = add if acc is None else acc + add
            total.append(acc)
        return total

    def synthesize_vorticity(first, count):
        def pairs(i, carry):
            for n in range(4):
                q = first + 8 * i + 2 * n
                rhs = jnp.concatenate([held[q], held[q + 1]], axis=1)
                grid = jnp.dot(table_ref[...], rhs, preferred_element_type=F32)
                vort_ref[q] = grid[:, :GROUP].astype(BF16)
                vort_ref[q + 1] = grid[:, GROUP:].astype(BF16)
            return carry

        lax.fori_loop(0, count // 8, pairs, 0)

    def begin_last():
        def columns_tile(n, inner):
            early_last[n, 0], early_last[n, 1] = product(full, slots - 1, None, n, (0,))
            return inner

        lax.fori_loop(0, tiles, columns_tile, 0)

    def begin(g, s, part=None):
        for i in (1, 2):
            gather_copy(g, i, part).wait_recv()

        def columns_tile(n, inner):
            if part is None:
                early[n, 0], early[n, 1] = product(g, s, part, n, (0, 1, 3))
            else:
                piece = slice(part * narrow, (part + 1) * narrow)
                more = product(g, s, part, n, (1, 3))
                for p in range(2):
                    early_last[n, p, piece] += more[p]
            return inner

        lax.fori_loop(0, tiles, columns_tile, 0)

    def multiply(g, s, part=None):
        for i in (4, 5):
            gather_copy(g, i, part).wait_recv()

        def columns_tile(turn, inner):
            n = lax.rem(turn + wave, tiles)
            total = product(g, s, part, n, (2,))
            if part is None:
                total = [total[p] + early[n, p] for p in range(2)]
            else:
                piece = slice(part * narrow, (part + 1) * narrow)
                total = [total[p] + early_last[n, p, piece] for p in range(2)]
            for at, value in ((0, total[0] + total[1]), (half, total[0] - total[1])):
                if part is None:
                    sb[g, pl.ds(at + n * per, per)] = value.T.astype(BF16).reshape(per, rows, GROUP)
                else:
                    turned = value.T.reshape(per, rows, narrow)
                    packed = jnp.concatenate([turned[:, :short], turned[:, short:]], axis=2)
                    sb[g, pl.ds(at + n * per, per), part * short : (part + 1) * short] = packed.astype(BF16)

            def send(i, after):
                peer = n * per + lax.rem(i, per) + half * (i // per)

                @pl.when(peer != wave)
                def _():
                    pltpu.make_async_remote_copy(
                        src_ref=sb.at[g, peer, lines(part)],
                        dst_ref=rv.at[g, wave, lines(part)],
                        send_sem=as_sem.at[g + (part or 0)],
                        recv_sem=ar_sem.at[g + (part or 0)],
                        device_id=(peer, lat),
                        device_id_type=MESH,
                    ).start()

                return after

            lax.fori_loop(0, 2 * per, send, 0)
            return inner

        lax.fori_loop(0, tiles, columns_tile, 0)
        self_copy(g, part).start()

    def hand_on(g, part=None):
        gather_copy(g, 0, part).wait_recv()
        gather_copy(g, 4, part).start()
        gather_copy(g, 3, part).wait_recv()
        gather_copy(g, 5, part).start()

    numbers.wait()
    prepare(0)
    pl.semaphore_wait(barrier, waves + 1)
    start_own(0)
    for s in range(1, slots):
        prepare(s)
    make_table()
    hand_on(0)
    start_own(1)
    leg_copy(0).wait()
    begin(0, 0)

    def step(g, carry):
        @pl.when(g + 1 < full)
        def _():
            hand_on(g + 1)

        @pl.when(g + 2 < full)
        def _():
            start_own(g + 2)

        @pl.when(g + 2 == full)
        def _():
            start_own(full, 0)

        @pl.when(g + 1 == full)
        def _():
            hand_on(full, 0)
            start_own(full, 1)

        multiply(g, lax.rem(g, slots))

        @pl.when(g == slots + 1)
        def _():
            synthesize_vorticity(rows // 2, rows // 2)

        @pl.when(g + 1 < slots)
        def _():
            leg_copy(g + 1).wait()

        @pl.when(g + 1 < full)
        def _():
            begin(g + 1, lax.rem(g + 1, slots))

        @pl.when(g + 2 == full)
        def _():
            begin_last()

        @pl.when((g >= 1) & (g < full - 1))
        def _():
            arrange(g - 1)

        @pl.when(g == slots)
        def _():
            synthesize_vorticity(0, rows // 2)

        return carry

    lax.fori_loop(0, full, step, 0)
    begin(full, slots - 1, 0)
    hand_on(full, 1)
    multiply(full, slots - 1, 0)
    begin(full, slots - 1, 1)
    multiply(full, slots - 1, 1)
    for g in (full - 2, full - 1):
        arrange(g)
    for part in range(2):
        arrange_half(part)

    def finish(g, carry):
        for i in range(6):
            gather_copy(g, i).wait_send()
        all_of(g).wait_send()
        return carry

    lax.fori_loop(0, full, finish, 0)
    for part in range(2):
        for i in range(6):
            gather_copy(full, i, part).wait_send()
        all_of(full, part).wait_send()


def synthesis_kernel(block, table_ref, wind_ref, vort_ref, out_ref, made, out_sem):
    rows = wind_ref.shape[0]

    def out_copy(i):
        piece = pl.ds(i * block, block)
        return pltpu.make_async_copy(made.at[piece], out_ref.at[piece], out_sem.at[i])

    for q in range(0, rows, 2):
        rhs = jnp.concatenate([wind_ref[q], wind_ref[q + 1]], axis=1)
        grid = jnp.dot(table_ref[...], rhs, preferred_element_type=F32)
        made[q] = (vort_ref[q].astype(F32) * grid[:, :GROUP]).astype(BF16)
        made[q + 1] = (vort_ref[q + 1].astype(F32) * grid[:, GROUP:]).astype(BF16)
        if (q + 2) % block == 0:
            out_copy(q // block).start()

    def finish(i, carry):
        out_copy(i).wait()
        return carry

    lax.fori_loop(0, rows // block, finish, 0)


def shards(waves, spectral, legendre, wavenumber):
    spectral = jnp.swapaxes(spectral, 3, 4)
    slots = spectral.shape[1]
    depth = spectral.shape[4]
    rows = 2 * legendre.shape[3] // waves
    band = legendre.shape[3]
    tiles = max(1, band // 256)
    chunks = 3 * slots
    inner = 2 * slots * waves

    table, wind, vort = pl.pallas_call(
        functools.partial(exchange_kernel, waves),
        out_shape=[
            jax.ShapeDtypeStruct((NLONW, inner), BF16),
            jax.ShapeDtypeStruct((rows, inner, GROUP), BF16),
            jax.ShapeDtypeStruct((rows, NLONW, GROUP), BF16),
        ],
        in_specs=[
            pl.BlockSpec(memory_space=pl.ANY),
            pl.BlockSpec(memory_space=pltpu.VMEM),
            pl.BlockSpec(memory_space=pl.ANY),
        ],
        out_specs=[pl.BlockSpec(memory_space=pltpu.VMEM)] * 3,
        scratch_shapes=[
            pltpu.VMEM((chunks, BANDS, 2, GROUP, depth), BF16),
            pltpu.VMEM(legendre.shape, BF16),
            pltpu.VMEM((chunks, waves, rows, GROUP), BF16),
            pltpu.VMEM((chunks, waves, rows, GROUP), BF16),
            pltpu.VMEM((waves * rows, GROUP), F32),
            pltpu.VMEM((tiles, 2, GROUP, band // tiles), F32),
            pltpu.VMEM((tiles, 2, GROUP, band // tiles), F32),
            pltpu.VMEM((rows, inner, GROUP), BF16),
            pltpu.SMEM((slots * waves,), jnp.int32),
            pltpu.SemaphoreType.DMA,
            pltpu.SemaphoreType.DMA((slots,)),
            pltpu.SemaphoreType.DMA((chunks + 1,)),
            pltpu.SemaphoreType.DMA((chunks + 1, 6)),
            pltpu.SemaphoreType.DMA((chunks + 1, 6)),
            pltpu.SemaphoreType.DMA((chunks + 1,)),
            pltpu.SemaphoreType.DMA((chunks + 1,)),
        ],
        compiler_params=pltpu.CompilerParams(
            collective_id=0, has_side_effects=True, vmem_limit_bytes=38 * 1024 * 1024
        ),
        name="gather_sum_exchange",
    )(wavenumber, spectral, legendre)

    block = 8
    flux = pl.pallas_call(
        functools.partial(synthesis_kernel, block),
        out_shape=jax.ShapeDtypeStruct((rows, NLONW, GROUP), BF16),
        in_specs=[pl.BlockSpec(memory_space=pltpu.VMEM)] * 3,
        out_specs=pl.BlockSpec(memory_space=pl.ANY),
        scratch_shapes=[
            pltpu.VMEM((rows, NLONW, GROUP), BF16),
            pltpu.SemaphoreType.DMA((rows // block,)),
        ],
        compiler_params=pltpu.CompilerParams(vmem_limit_bytes=24 * 1024 * 1024),
        name="synthesis_product",
    )(table, wind, vort)
    return flux[None]


def solution(mesh):
    return jax.shard_map(
        functools.partial(shards, mesh.shape["wave"]),
        mesh=mesh,
        in_specs=(P(None, "wave", None, "lat", None), P("wave", None, None, "lat"), P()),
        out_specs=P("lat", "wave", None, None),
        check_vma=False,
    )
```

```python
import functools
import math

import jax
import jax.numpy as jnp
from jax import lax
from jax.experimental import pallas as pl
from jax.experimental.pallas import tpu as pltpu
from jax.sharding import PartitionSpec as P

TRUNC = 7999
NLONW = 512
PERIOD = 2 * TRUNC + 2
MESH = pl.DeviceIdType.MESH
F32 = jnp.float32
BF16 = jnp.bfloat16
BANDS = 4
GROUP = 128


def exchange_kernel(
    waves, wn_hbm, spec_ref, leg_ref, table_ref, wind_ref, vort_ref,
    xg, leg_v, sb, rv, wide, early, early_last, held, wn_ref,
    wn_sem, leg_sem, own_sem, gs_sem, gr_sem, as_sem, ar_sem,
):
    wave = lax.axis_index("wave")
    lat = lax.axis_index("lat")
    plus, minus = lax.rem(lat + 1, BANDS), lax.rem(lat + BANDS - 1, BANDS)
    batches, slots, _, columns, depth = spec_ref.shape
    levels = columns // 6
    full = 3 * slots - 1
    rows = rv.shape[2]
    short = rows // 2
    narrow = GROUP // 2
    band = leg_ref.shape[3]
    tile = min(512, band)
    tiles = band // tile
    per = tile // rows
    half = waves // 2

    numbers = pltpu.make_async_copy(wn_hbm, wn_ref, wn_sem)
    numbers.start()

    def leg_copy(s):
        return pltpu.make_async_copy(leg_ref.at[s], leg_v.at[s], leg_sem.at[s])

    barrier = pltpu.get_barrier_semaphore()
    for other in (plus, minus):
        pl.semaphore_signal(barrier, inc=1, device_id=(wave, other), device_id_type=MESH)

    def greet(i, carry):
        peer = lax.rem(wave + i, waves)
        pl.semaphore_signal(barrier, inc=1, device_id=(peer, lat), device_id_type=MESH)
        return carry

    lax.fori_loop(1, waves, greet, 0)
    for s in range(slots):
        leg_copy(s).start()

    def prepare(s):
        first = wn_ref[wave * slots + s] + 2 * depth * lat
        slot_index = lax.broadcasted_iota(jnp.int32, (2 * levels, depth), 1)
        for p in range(2):
            live = first + p + 2 * slot_index <= TRUNC
            for b in range(batches):
                at = b * 2 * levels
                for r in range(2):
                    src = r * 3 * levels
                    vort = spec_ref[b, s, p, src : src + levels].astype(F32)
                    xg[s, 0, p, at + r * levels : at + (r + 1) * levels] = jnp.where(
                        live[:levels], vort, 0.0
                    ).astype(BF16)
                    wind = spec_ref[b, s, p, src + levels : src + 3 * levels].astype(F32)
                    xg[(1 + r) * slots + s, 0, p, at : at + 2 * levels] = jnp.where(live, wind, 0.0).astype(BF16)

    def gather_copy(g, i, part=None):
        src, dst, p, to = (
            (0, 3, 0, plus), (0, 3, 1, plus), (0, 1, 0, minus), (0, 1, 1, minus),
            (3, 2, 0, plus), (1, 2, 1, minus),
        )[i]
        piece = pl.ds(0, GROUP) if part is None else pl.ds(part * narrow, narrow)
        at = g if part is None else g + part
        return pltpu.make_async_remote_copy(
            src_ref=xg.at[g, src, p, piece],
            dst_ref=xg.at[g, dst, p, piece],
            send_sem=gs_sem.at[at, i],
            recv_sem=gr_sem.at[at, i],
            device_id=(wave, to),
            device_id_type=MESH,
        )

    def start_own(g, part=None):
        for i in (0, 3, 1, 2):
            gather_copy(g, i, part).start()

    def lines(part):
        return pl.ds(0, rows) if part is None else pl.ds(part * short, short)

    def self_copy(g, part=None):
        return pltpu.make_async_copy(
            sb.at[g, wave, lines(part)], rv.at[g, wave, lines(part)], own_sem.at[g + (part or 0)]
        )

    def all_of(g, part=None):
        peer = lax.rem(wave + 1, waves)
        return pltpu.make_async_remote_copy(
            src_ref=sb.at[g, pl.ds(0, waves - 1), lines(part)],
            dst_ref=rv.at[g, pl.ds(0, waves - 1), lines(part)],
            send_sem=as_sem.at[g + (part or 0)],
            recv_sem=ar_sem.at[g + (part or 0)],
            device_id=(peer, lat),
            device_id_type=MESH,
        )

    def make_table():
        lane = lax.broadcasted_iota(jnp.int32, (8, 2 * slots * waves), 1)
        slot = slots * lax.rem(lane, waves) + lax.rem(lane // waves, slots)
        number = jnp.zeros_like(lane)
        for n in range(slots * waves):
            number = jnp.where(slot == n, wn_ref[n], number)
        weight = jnp.where(number == 0, 1.0, 2.0).astype(F32)
        real = lane < slots * waves

        def block(i, carry):
            column = lax.broadcasted_iota(jnp.int32, lane.shape, 0)
            parts = []
            for n in range(2):
                product = number * (column + (16 * i + 8 * n))
                turns = jnp.floor(product.astype(F32) * (1.0 / PERIOD)).astype(jnp.int32)
                phase = product - turns * PERIOD
                phase = jnp.where(phase < 0, phase + PERIOD, phase)
                phase = jnp.where(phase >= PERIOD, phase - PERIOD, phase)
                angle = phase.astype(F32) * (2.0 * math.pi / PERIOD)
                parts.append(jnp.where(real, weight * jnp.cos(angle), -weight * jnp.sin(angle)))
            table_ref[pl.ds(pl.multiple_of(16 * i, 16), 16), :] = jnp.concatenate(parts, axis=0).astype(BF16)
            return carry

        lax.fori_loop(0, NLONW // 16, block, 0)

    def arrange(g):
        s = lax.rem(g, slots)
        t = g // slots
        all_of(g).wait_recv()
        self_copy(g).wait()
        wide[...] = rv[g].astype(F32).reshape(waves * rows, GROUP)

        @pl.when(t == 0)
        def _():
            lane = lax.broadcasted_iota(jnp.int32, (waves, GROUP), 1)
            real_lane = lax.rem(lane // levels, 2) == 0

            def latitude(q, carry):
                x = wide[pl.ds(q, waves, stride=rows), :]
                real = jnp.where(real_lane, x, pltpu.roll(x, levels, 1))
                imag = jnp.where(real_lane, pltpu.roll(x, GROUP - levels, 1), x)
                held[q, pl.ds(s * waves, waves), :] = real.astype(BF16)
                held[q, pl.ds((slots + s) * waves, waves), :] = imag.astype(BF16)
                return carry

            lax.fori_loop(0, rows, latitude, 0, unroll=8)

        @pl.when(t > 0)
        def _():
            def latitude(q, carry):
                x = wide[pl.ds(q, waves, stride=rows), :]
                wind_ref[q, pl.ds((g - slots) * waves, waves), :] = x.astype(BF16)
                return carry

            lax.fori_loop(0, rows, latitude, 0, unroll=8)

    def arrange_half(part):
        all_of(full, part).wait_recv()
        self_copy(full, part).wait()
        wide[0 : waves * short] = rv[full, :, part * short : (part + 1) * short].astype(F32).reshape(
            waves * short, GROUP
        )
        at = pl.ds((full - slots) * waves, waves)

        def latitude(q, carry):
            x = wide[pl.ds(q, waves, stride=short), :]
            turned = pltpu.roll(x, narrow, 1)
            first, second = (x, turned) if part == 0 else (turned, x)
            cut = slice(part * narrow, (part + 1) * narrow)
            wind_ref[q, at, cut] = first[:, cut].astype(BF16)
            wind_ref[q + short, at, cut] = second[:, cut].astype(BF16)
            return carry

        lax.fori_loop(0, short, latitude, 0, unroll=8)

    def product(g, s, part, n, sources):
        piece = slice(0, GROUP) if part is None else slice(part * narrow, (part + 1) * narrow)
        total = []
        for p in range(2):
            acc = None
            for j in sources:
                k0 = pl.multiple_of(lax.rem(lat + j, BANDS) * depth, depth)
                poly = leg_v[s, p, pl.ds(k0, depth), pl.ds(pl.multiple_of(n * tile, tile), tile)]
                add = jnp.dot(xg[g, j, p, piece], poly, preferred_element_type=F32)
                acc = add if acc is None else acc + add
            total.append(acc)
        return total

    def synthesize_vorticity(first, count):
        def pairs(i, carry):
            for n in range(4):
                q = first + 8 * i + 2 * n
                rhs = jnp.concatenate([held[q], held[q + 1]], axis=1)
                grid = jnp.dot(table_ref[...], rhs, preferred_element_type=F32)
                vort_ref[q] = grid[:, :GROUP].astype(BF16)
                vort_ref[q + 1] = grid[:, GROUP:].astype(BF16)
            return carry

        lax.fori_loop(0, count // 8, pairs, 0)

    def begin_last():
        def columns_tile(n, inner):
            early_last[n, 0], early_last[n, 1] = product(full, slots - 1, None, n, (0,))
            return inner

        lax.fori_loop(0, tiles, columns_tile, 0)

    def begin(g, s, part=None):
        for i in (1, 2):
            gather_copy(g, i, part).wait_recv()

        def columns_tile(n, inner):
            if part is None:
                early[n, 0], early[n, 1] = product(g, s, part, n, (0, 1, 3))
            else:
                piece = slice(part * narrow, (part + 1) * narrow)
                more = product(g, s, part, n, (1, 3))
                for p in range(2):
                    early_last[n, p, piece] += more[p]
            return inner

        lax.fori_loop(0, tiles, columns_tile, 0)

    def multiply(g, s, part=None):
        for i in (4, 5):
            gather_copy(g, i, part).wait_recv()

        def columns_tile(turn, inner):
            n = lax.rem(turn + wave, tiles)
            total = product(g, s, part, n, (2,))
            if part is None:
                total = [total[p] + early[n, p] for p in range(2)]
            else:
                piece = slice(part * narrow, (part + 1) * narrow)
                total = [total[p] + early_last[n, p, piece] for p in range(2)]
            for at, value in ((0, total[0] + total[1]), (half, total[0] - total[1])):
                if part is None:
                    sb[g, pl.ds(at + n * per, per)] = value.T.astype(BF16).reshape(per, rows, GROUP)
                else:
                    turned = value.T.reshape(per, rows, narrow)
                    packed = jnp.concatenate([turned[:, :short], turned[:, short:]], axis=2)
                    sb[g, pl.ds(at + n * per, per), part * short : (part + 1) * short] = packed.astype(BF16)

            def send(i, after):
                peer = n * per + lax.rem(i, per) + half * (i // per)

                @pl.when(peer != wave)
                def _():
                    pltpu.make_async_remote_copy(
                        src_ref=sb.at[g, peer, lines(part)],
                        dst_ref=rv.at[g, wave, lines(part)],
                        send_sem=as_sem.at[g + (part or 0)],
                        recv_sem=ar_sem.at[g + (part or 0)],
                        device_id=(peer, lat),
                        device_id_type=MESH,
                    ).start()

                return after

            lax.fori_loop(0, 2 * per, send, 0)
            return inner

        lax.fori_loop(0, tiles, columns_tile, 0)
        self_copy(g, part).start()

    def hand_on(g, part=None):
        gather_copy(g, 0, part).wait_recv()
        gather_copy(g, 4, part).start()
        gather_copy(g, 3, part).wait_recv()
        gather_copy(g, 5, part).start()

    numbers.wait()
    prepare(0)
    pl.semaphore_wait(barrier, waves + 1)
    start_own(0)
    for s in range(1, slots):
        prepare(s)
    make_table()
    hand_on(0)
    start_own(1)
    leg_copy(0).wait()
    begin(0, 0)

    def step(g, carry):
        @pl.when(g + 1 < full)
        def _():
            hand_on(g + 1)

        @pl.when(g + 2 < full)
        def _():
            start_own(g + 2)

        @pl.when(g + 2 == full)
        def _():
            start_own(full, 0)

        @pl.when(g + 1 == full)
        def _():
            hand_on(full, 0)
            start_own(full, 1)

        multiply(g, lax.rem(g, slots))

        @pl.when(g == slots + 1)
        def _():
            synthesize_vorticity(rows // 2, rows // 2)

        @pl.when(g + 1 < slots)
        def _():
            leg_copy(g + 1).wait()

        @pl.when(g + 1 < full)
        def _():
            begin(g + 1, lax.rem(g + 1, slots))

        @pl.when(g + 2 == full)
        def _():
            begin_last()

        @pl.when((g >= 1) & (g < full - 1))
        def _():
            arrange(g - 1)

        @pl.when(g == slots)
        def _():
            synthesize_vorticity(0, rows // 2)

        return carry

    lax.fori_loop(0, full, step, 0)
    begin(full, slots - 1, 0)
    hand_on(full, 1)
    multiply(full, slots - 1, 0)
    begin(full, slots - 1, 1)
    multiply(full, slots - 1, 1)
    for g in (full - 2, full - 1):
        arrange(g)
    for part in range(2):
        arrange_half(part)

    def finish(g, carry):
        for i in range(6):
            gather_copy(g, i).wait_send()
        all_of(g).wait_send()
        return carry

    lax.fori_loop(0, full, finish, 0)
    for part in range(2):
        for i in range(6):
            gather_copy(full, i, part).wait_send()
        all_of(full, part).wait_send()


def synthesis_kernel(block, table_ref, wind_ref, vort_ref, out_ref, made, out_sem):
    rows = wind_ref.shape[0]

    def out_copy(i):
        piece = pl.ds(i * block, block)
        return pltpu.make_async_copy(made.at[piece], out_ref.at[piece], out_sem.at[i])

    for q in range(0, rows, 2):
        rhs = jnp.concatenate([wind_ref[q], wind_ref[q + 1]], axis=1)
        grid = jnp.dot(table_ref[...], rhs, preferred_element_type=F32)
        made[q] = (vort_ref[q].astype(F32) * grid[:, :GROUP]).astype(BF16)
        made[q + 1] = (vort_ref[q + 1].astype(F32) * grid[:, GROUP:]).astype(BF16)
        if (q + 2) % block == 0:
            out_copy(q // block).start()

    def finish(i, carry):
        out_copy(i).wait()
        return carry

    lax.fori_loop(0, rows // block, finish, 0)


def shards(waves, spectral, legendre, wavenumber):
    spectral = jnp.swapaxes(spectral, 3, 4)
    slots = spectral.shape[1]
    depth = spectral.shape[4]
    rows = 2 * legendre.shape[3] // waves
    band = legendre.shape[3]
    tiles = max(1, band // 512)
    chunks = 3 * slots
    inner = 2 * slots * waves

    table, wind, vort = pl.pallas_call(
        functools.partial(exchange_kernel, waves),
        out_shape=[
            jax.ShapeDtypeStruct((NLONW, inner), BF16),
            jax.ShapeDtypeStruct((rows, inner, GROUP), BF16),
            jax.ShapeDtypeStruct((rows, NLONW, GROUP), BF16),
        ],
        in_specs=[
            pl.BlockSpec(memory_space=pl.ANY),
            pl.BlockSpec(memory_space=pltpu.VMEM),
            pl.BlockSpec(memory_space=pl.ANY),
        ],
        out_specs=[pl.BlockSpec(memory_space=pltpu.VMEM)] * 3,
        scratch_shapes=[
            pltpu.VMEM((chunks, BANDS, 2, GROUP, depth), BF16),
            pltpu.VMEM(legendre.shape, BF16),
            pltpu.VMEM((chunks, waves, rows, GROUP), BF16),
            pltpu.VMEM((chunks, waves, rows, GROUP), BF16),
            pltpu.VMEM((waves * rows, GROUP), F32),
            pltpu.VMEM((tiles, 2, GROUP, band // tiles), F32),
            pltpu.VMEM((tiles, 2, GROUP, band // tiles), F32),
            pltpu.VMEM((rows, inner, GROUP), BF16),
            pltpu.SMEM((slots * waves,), jnp.int32),
            pltpu.SemaphoreType.DMA,
            pltpu.SemaphoreType.DMA((slots,)),
            pltpu.SemaphoreType.DMA((chunks + 1,)),
            pltpu.SemaphoreType.DMA((chunks + 1, 6)),
            pltpu.SemaphoreType.DMA((chunks + 1, 6)),
            pltpu.SemaphoreType.DMA((chunks + 1,)),
            pltpu.SemaphoreType.DMA((chunks + 1,)),
        ],
        compiler_params=pltpu.CompilerParams(
            collective_id=0, has_side_effects=True, vmem_limit_bytes=38 * 1024 * 1024
        ),
        name="gather_sum_exchange",
    )(wavenumber, spectral, legendre)

    block = 8
    flux = pl.pallas_call(
        functools.partial(synthesis_kernel, block),
        out_shape=jax.ShapeDtypeStruct((rows, NLONW, GROUP), BF16),
        in_specs=[pl.BlockSpec(memory_space=pltpu.VMEM)] * 3,
        out_specs=pl.BlockSpec(memory_space=pl.ANY),
        scratch_shapes=[
            pltpu.VMEM((rows, NLONW, GROUP), BF16),
            pltpu.SemaphoreType.DMA((rows // block,)),
        ],
        compiler_params=pltpu.CompilerParams(vmem_limit_bytes=24 * 1024 * 1024),
        name="synthesis_product",
    )(table, wind, vort)
    return flux[None]


def solution(mesh):
    return jax.shard_map(
        functools.partial(shards, mesh.shape["wave"]),
        mesh=mesh,
        in_specs=(P(None, "wave", None, "lat", None), P("wave", None, None, "lat"), P()),
        out_specs=P("lat", "wave", None, None),
        check_vma=False,
    )
```

```python
import functools
import math

import jax
import jax.numpy as jnp
from jax import lax
from jax.experimental import pallas as pl
from jax.experimental.pallas import tpu as pltpu
from jax.sharding import PartitionSpec as P

TRUNC = 7999
NLONW = 512
PERIOD = 2 * TRUNC + 2
MESH = pl.DeviceIdType.MESH
F32 = jnp.float32
BF16 = jnp.bfloat16
BANDS = 4
GROUP = 128


def exchange_kernel(
    waves, wn_hbm, spec_ref, leg_ref, table_ref, wind_ref, vort_ref,
    xg, leg_v, sb, rv, wide, early, early_last, held, wn_ref,
    wn_sem, leg_sem, own_sem, gs_sem, gr_sem, as_sem, ar_sem,
):
    wave = lax.axis_index("wave")
    lat = lax.axis_index("lat")
    plus, minus = lax.rem(lat + 1, BANDS), lax.rem(lat + BANDS - 1, BANDS)
    batches, slots, _, columns, depth = spec_ref.shape
    levels = columns // 6
    full = 3 * slots - 1
    rows = rv.shape[2]
    short = rows // 2
    narrow = GROUP // 2
    band = leg_ref.shape[3]
    tile = min(512, band)
    tiles = band // tile
    per = tile // rows
    half = waves // 2

    numbers = pltpu.make_async_copy(wn_hbm, wn_ref, wn_sem)
    numbers.start()

    def leg_copy(s):
        return pltpu.make_async_copy(leg_ref.at[s], leg_v.at[s], leg_sem.at[s])

    barrier = pltpu.get_barrier_semaphore()
    for other in (plus, minus):
        pl.semaphore_signal(barrier, inc=1, device_id=(wave, other), device_id_type=MESH)

    def greet(i, carry):
        peer = lax.rem(wave + i, waves)
        pl.semaphore_signal(barrier, inc=1, device_id=(peer, lat), device_id_type=MESH)
        return carry

    lax.fori_loop(1, waves, greet, 0)
    for s in range(slots):
        leg_copy(s).start()

    def prepare(s, winds):
        first = wn_ref[wave * slots + s] + 2 * depth * lat
        slot_index = lax.broadcasted_iota(jnp.int32, (2 * levels, depth), 1)
        for p in range(2):
            live = first + p + 2 * slot_index <= TRUNC
            for b in range(batches):
                at = b * 2 * levels
                for r in range(2):
                    src = r * 3 * levels
                    if winds:
                        wind = spec_ref[b, s, p, src + levels : src + 3 * levels].astype(F32)
                        xg[(1 + r) * slots + s, 0, p, at : at + 2 * levels] = jnp.where(live, wind, 0.0).astype(BF16)
                    else:
                        vort = spec_ref[b, s, p, src : src + levels].astype(F32)
                        xg[s, 0, p, at + r * levels : at + (r + 1) * levels] = jnp.where(
                            live[:levels], vort, 0.0
                        ).astype(BF16)

    def gather_copy(g, i, part=None):
        src, dst, p, to = (
            (0, 3, 0, plus), (0, 3, 1, plus), (0, 1, 0, minus), (0, 1, 1, minus),
            (3, 2, 0, plus), (1, 2, 1, minus),
        )[i]
        piece = pl.ds(0, GROUP) if part is None else pl.ds(part * narrow, narrow)
        at = g if part is None else g + part
        return pltpu.make_async_remote_copy(
            src_ref=xg.at[g, src, p, piece],
            dst_ref=xg.at[g, dst, p, piece],
            send_sem=gs_sem.at[at, i],
            recv_sem=gr_sem.at[at, i],
            device_id=(wave, to),
            device_id_type=MESH,
        )

    def start_own(g, part=None):
        for i in (0, 3, 1, 2):
            gather_copy(g, i, part).start()

    def lines(part):
        return pl.ds(0, rows) if part is None else pl.ds(part * short, short)

    def self_copy(g, part=None):
        return pltpu.make_async_copy(
            sb.at[g, wave, lines(part)], rv.at[g, wave, lines(part)], own_sem.at[g + (part or 0)]
        )

    def all_of(g, part=None):
        peer = lax.rem(wave + 1, waves)
        return pltpu.make_async_remote_copy(
            src_ref=sb.at[g, pl.ds(0, waves - 1), lines(part)],
            dst_ref=rv.at[g, pl.ds(0, waves - 1), lines(part)],
            send_sem=as_sem.at[g + (part or 0)],
            recv_sem=ar_sem.at[g + (part or 0)],
            device_id=(peer, lat),
            device_id_type=MESH,
        )

    def make_table():
        lane = lax.broadcasted_iota(jnp.int32, (8, 2 * slots * waves), 1)
        slot = slots * lax.rem(lane, waves) + lax.rem(lane // waves, slots)
        number = jnp.zeros_like(lane)
        for n in range(slots * waves):
            number = jnp.where(slot == n, wn_ref[n], number)
        weight = jnp.where(number == 0, 1.0, 2.0).astype(F32)
        real = lane < slots * waves

        def block(i, carry):
            column = lax.broadcasted_iota(jnp.int32, lane.shape, 0)
            parts = []
            for n in range(2):
                product = number * (column + (16 * i + 8 * n))
                turns = jnp.floor(product.astype(F32) * (1.0 / PERIOD)).astype(jnp.int32)
                phase = product - turns * PERIOD
                phase = jnp.where(phase < 0, phase + PERIOD, phase)
                phase = jnp.where(phase >= PERIOD, phase - PERIOD, phase)
                angle = phase.astype(F32) * (2.0 * math.pi / PERIOD)
                parts.append(jnp.where(real, weight * jnp.cos(angle), -weight * jnp.sin(angle)))
            table_ref[pl.ds(pl.multiple_of(16 * i, 16), 16), :] = jnp.concatenate(parts, axis=0).astype(BF16)
            return carry

        lax.fori_loop(0, NLONW // 16, block, 0)

    def arrange(g):
        s = lax.rem(g, slots)
        t = g // slots
        all_of(g).wait_recv()
        self_copy(g).wait()
        wide[...] = rv[g].astype(F32).reshape(waves * rows, GROUP)

        @pl.when(t == 0)
        def _():
            lane = lax.broadcasted_iota(jnp.int32, (waves, GROUP), 1)
            real_lane = lax.rem(lane // levels, 2) == 0

            def latitude(q, carry):
                x = wide[pl.ds(q, waves, stride=rows), :]
                real = jnp.where(real_lane, x, pltpu.roll(x, levels, 1))
                imag = jnp.where(real_lane, pltpu.roll(x, GROUP - levels, 1), x)
                held[q, pl.ds(s * waves, waves), :] = real.astype(BF16)
                held[q, pl.ds((slots + s) * waves, waves), :] = imag.astype(BF16)
                return carry

            lax.fori_loop(0, rows, latitude, 0, unroll=8)

        @pl.when(t > 0)
        def _():
            def latitude(q, carry):
                x = wide[pl.ds(q, waves, stride=rows), :]
                wind_ref[q, pl.ds((g - slots) * waves, waves), :] = x.astype(BF16)
                return carry

            lax.fori_loop(0, rows, latitude, 0, unroll=8)

    def arrange_half(part):
        all_of(full, part).wait_recv()
        self_copy(full, part).wait()
        wide[0 : waves * short] = rv[full, :, part * short : (part + 1) * short].astype(F32).reshape(
            waves * short, GROUP
        )
        at = pl.ds((full - slots) * waves, waves)

        def latitude(q, carry):
            x = wide[pl.ds(q, waves, stride=short), :]
            turned = pltpu.roll(x, narrow, 1)
            first, second = (x, turned) if part == 0 else (turned, x)
            cut = slice(part * narrow, (part + 1) * narrow)
            wind_ref[q, at, cut] = first[:, cut].astype(BF16)
            wind_ref[q + short, at, cut] = second[:, cut].astype(BF16)
            return carry

        lax.fori_loop(0, short, latitude, 0, unroll=8)

    def product(g, s, part, n, sources):
        piece = slice(0, GROUP) if part is None else slice(part * narrow, (part + 1) * narrow)
        total = []
        for p in range(2):
            acc = None
            for j in sources:
                k0 = pl.multiple_of(lax.rem(lat + j, BANDS) * depth, depth)
                poly = leg_v[s, p, pl.ds(k0, depth), pl.ds(pl.multiple_of(n * tile, tile), tile)]
                add = jnp.dot(xg[g, j, p, piece], poly, preferred_element_type=F32)
                acc = add if acc is None else acc + add
            total.append(acc)
        return total

    def synthesize_vorticity(first, count):
        def pairs(i, carry):
            for n in range(4):
                q = first + 8 * i + 2 * n
                rhs = jnp.concatenate([held[q], held[q + 1]], axis=1)
                grid = jnp.dot(table_ref[...], rhs, preferred_element_type=F32)
                vort_ref[q] = grid[:, :GROUP].astype(BF16)
                vort_ref[q + 1] = grid[:, GROUP:].astype(BF16)
            return carry

        lax.fori_loop(0, count // 8, pairs, 0)

    def begin_last():
        def columns_tile(n, inner):
            early_last[n, 0], early_last[n, 1] = product(full, slots - 1, None, n, (0,))
            return inner

        lax.fori_loop(0, tiles, columns_tile, 0)

    def begin(g, s, part=None):
        for i in (1, 2):
            gather_copy(g, i, part).wait_recv()

        def columns_tile(n, inner):
            if part is None:
                early[n, 0], early[n, 1] = product(g, s, part, n, (0, 1, 3))
            else:
                piece = slice(part * narrow, (part + 1) * narrow)
                more = product(g, s, part, n, (1, 3))
                for p in range(2):
                    early_last[n, p, piece] += more[p]
            return inner

        lax.fori_loop(0, tiles, columns_tile, 0)

    def multiply(g, s, part=None):
        for i in (4, 5):
            gather_copy(g, i, part).wait_recv()

        def columns_tile(turn, inner):
            n = lax.rem(turn + wave, tiles)
            total = product(g, s, part, n, (2,))
            if part is None:
                total = [total[p] + early[n, p] for p in range(2)]
            else:
                piece = slice(part * narrow, (part + 1) * narrow)
                total = [total[p] + early_last[n, p, piece] for p in range(2)]
            for at, value in ((0, total[0] + total[1]), (half, total[0] - total[1])):
                if part is None:
                    sb[g, pl.ds(at + n * per, per)] = value.T.astype(BF16).reshape(per, rows, GROUP)
                else:
                    turned = value.T.reshape(per, rows, narrow)
                    packed = jnp.concatenate([turned[:, :short], turned[:, short:]], axis=2)
                    sb[g, pl.ds(at + n * per, per), part * short : (part + 1) * short] = packed.astype(BF16)

            def send(i, after):
                peer = n * per + lax.rem(i, per) + half * (i // per)

                @pl.when(peer != wave)
                def _():
                    pltpu.make_async_remote_copy(
                        src_ref=sb.at[g, peer, lines(part)],
                        dst_ref=rv.at[g, wave, lines(part)],
                        send_sem=as_sem.at[g + (part or 0)],
                        recv_sem=ar_sem.at[g + (part or 0)],
                        device_id=(peer, lat),
                        device_id_type=MESH,
                    ).start()

                return after

            lax.fori_loop(0, 2 * per, send, 0)
            return inner

        lax.fori_loop(0, tiles, columns_tile, 0)
        self_copy(g, part).start()

    def hand_on(g, part=None):
        gather_copy(g, 0, part).wait_recv()
        gather_copy(g, 4, part).start()
        gather_copy(g, 3, part).wait_recv()
        gather_copy(g, 5, part).start()

    numbers.wait()
    prepare(0, False)
    pl.semaphore_wait(barrier, waves + 1)
    start_own(0)
    for s in range(1, slots):
        prepare(s, False)
    for s in range(slots):
        prepare(s, True)
    make_table()
    hand_on(0)
    start_own(1)
    leg_copy(0).wait()
    begin(0, 0)

    def step(g, carry):
        @pl.when(g + 1 < full)
        def _():
            hand_on(g + 1)

        @pl.when(g + 2 < full)
        def _():
            start_own(g + 2)

        @pl.when(g + 2 == full)
        def _():
            start_own(full, 0)

        @pl.when(g + 1 == full)
        def _():
            hand_on(full, 0)
            start_own(full, 1)

        multiply(g, lax.rem(g, slots))

        @pl.when(g == slots + 1)
        def _():
            synthesize_vorticity(rows // 2, rows // 2)

        @pl.when(g + 1 < slots)
        def _():
            leg_copy(g + 1).wait()

        @pl.when(g + 1 < full)
        def _():
            begin(g + 1, lax.rem(g + 1, slots))

        @pl.when(g + 2 == full)
        def _():
            begin_last()

        @pl.when((g >= 1) & (g < full - 1))
        def _():
            arrange(g - 1)

        @pl.when(g == slots)
        def _():
            synthesize_vorticity(0, rows // 2)

        return carry

    lax.fori_loop(0, full, step, 0)
    begin(full, slots - 1, 0)
    hand_on(full, 1)
    multiply(full, slots - 1, 0)
    begin(full, slots - 1, 1)
    multiply(full, slots - 1, 1)
    for g in (full - 2, full - 1):
        arrange(g)

    def finish(g, carry):
        for i in range(6):
            gather_copy(g, i).wait_send()
        all_of(g).wait_send()
        return carry

    lax.fori_loop(0, full, finish, 0)
    for part in range(2):
        for i in range(6):
            gather_copy(full, i, part).wait_send()
    all_of(full, 0).wait_send()
    for part in range(2):
        arrange_half(part)
    all_of(full, 1).wait_send()


def synthesis_kernel(block, table_ref, wind_ref, vort_ref, out_ref, made, out_sem):
    rows = wind_ref.shape[0]

    def out_copy(i):
        piece = pl.ds(i * block, block)
        return pltpu.make_async_copy(made.at[piece], out_ref.at[piece], out_sem.at[i])

    for q in range(0, rows, 2):
        rhs = jnp.concatenate([wind_ref[q], wind_ref[q + 1]], axis=1)
        grid = jnp.dot(table_ref[...], rhs, preferred_element_type=F32)
        made[q] = (vort_ref[q].astype(F32) * grid[:, :GROUP]).astype(BF16)
        made[q + 1] = (vort_ref[q + 1].astype(F32) * grid[:, GROUP:]).astype(BF16)
        if (q + 2) % block == 0:
            out_copy(q // block).start()

    def finish(i, carry):
        out_copy(i).wait()
        return carry

    lax.fori_loop(0, rows // block, finish, 0)


def shards(waves, spectral, legendre, wavenumber):
    spectral = jnp.swapaxes(spectral, 3, 4)
    slots = spectral.shape[1]
    depth = spectral.shape[4]
    rows = 2 * legendre.shape[3] // waves
    band = legendre.shape[3]
    tiles = max(1, band // 512)
    chunks = 3 * slots
    inner = 2 * slots * waves

    table, wind, vort = pl.pallas_call(
        functools.partial(exchange_kernel, waves),
        out_shape=[
            jax.ShapeDtypeStruct((NLONW, inner), BF16),
            jax.ShapeDtypeStruct((rows, inner, GROUP), BF16),
            jax.ShapeDtypeStruct((rows, NLONW, GROUP), BF16),
        ],
        in_specs=[
            pl.BlockSpec(memory_space=pl.ANY),
            pl.BlockSpec(memory_space=pltpu.VMEM),
            pl.BlockSpec(memory_space=pl.ANY),
        ],
        out_specs=[pl.BlockSpec(memory_space=pltpu.VMEM)] * 3,
        scratch_shapes=[
            pltpu.VMEM((chunks, BANDS, 2, GROUP, depth), BF16),
            pltpu.VMEM(legendre.shape, BF16),
            pltpu.VMEM((chunks, waves, rows, GROUP), BF16),
            pltpu.VMEM((chunks, waves, rows, GROUP), BF16),
            pltpu.VMEM((waves * rows, GROUP), F32),
            pltpu.VMEM((tiles, 2, GROUP, band // tiles), F32),
            pltpu.VMEM((tiles, 2, GROUP, band // tiles), F32),
            pltpu.VMEM((rows, inner, GROUP), BF16),
            pltpu.SMEM((slots * waves,), jnp.int32),
            pltpu.SemaphoreType.DMA,
            pltpu.SemaphoreType.DMA((slots,)),
            pltpu.SemaphoreType.DMA((chunks + 1,)),
            pltpu.SemaphoreType.DMA((chunks + 1, 6)),
            pltpu.SemaphoreType.DMA((chunks + 1, 6)),
            pltpu.SemaphoreType.DMA((chunks + 1,)),
            pltpu.SemaphoreType.DMA((chunks + 1,)),
        ],
        compiler_params=pltpu.CompilerParams(
            collective_id=0, has_side_effects=True, vmem_limit_bytes=38 * 1024 * 1024
        ),
        name="gather_sum_exchange",
    )(wavenumber, spectral, legendre)

    block = 4
    flux = pl.pallas_call(
        functools.partial(synthesis_kernel, block),
        out_shape=jax.ShapeDtypeStruct((rows, NLONW, GROUP), BF16),
        in_specs=[pl.BlockSpec(memory_space=pltpu.VMEM)] * 3,
        out_specs=pl.BlockSpec(memory_space=pl.ANY),
        scratch_shapes=[
            pltpu.VMEM((rows, NLONW, GROUP), BF16),
            pltpu.SemaphoreType.DMA((rows // block,)),
        ],
        compiler_params=pltpu.CompilerParams(vmem_limit_bytes=24 * 1024 * 1024),
        name="synthesis_product",
    )(table, wind, vort)
    return flux[None]


def solution(mesh):
    return jax.shard_map(
        functools.partial(shards, mesh.shape["wave"]),
        mesh=mesh,
        in_specs=(P(None, "wave", None, "lat", None), P("wave", None, None, "lat"), P()),
        out_specs=P("lat", "wave", None, None),
        check_vma=False,
    )
```
